32 devices in a mesh: shot: 4 (over y, x), space: 8 (over z, core).
Axes of the slice: x: 2, y: 2, z: 4, core: 2. Of those that a mesh axis runs over, the one named last changes fastest.
Arguments:
- residual: bfloat16 [4, 2048, 1536], P('shot', 'space'), may hold values from -6 to 6
- record_tile: int32 [4, 2048, 1], P('shot', 'space'), may hold values from 0 to 7; in each aligned block of 256 rows (0 to 255, 256 to 511, ..., all dimensions but the last counted through in order) at most 48 rows name the same one
- record_cell: int32 [4, 2048], P('shot', 'space'), may hold values from 0 to 1023
- time_filter: bfloat16 [6, 1536], replicated, may hold values from -0.15625 to 0.15625
- offsets: int32 [4], P('shot'), may hold values from 0 to 16
- velocity: float32 [4, 64, 128, 256], P('shot', None, 'space'), may hold values from 0.05 to 0.19
- adjoint_prev: float32 [4, 64, 128, 256], P('shot', None, 'space'), may hold values from -6 to 6
- adjoint_now: float32 [4, 64, 128, 256], P('shot', None, 'space'), may hold values from -6 to 6
- forward_accel: bfloat16 [4, 6, 64, 128, 256], P('shot', None, None, 'space'), may hold values from -6 to 6
Outputs:
- gradient: float32 [80, 128, 256], P('shot', 'space')
- adjoint_last: float32 [4, 64, 128, 256], P('shot', None, 'space')
The draws below stay inside these ranges and needn't reach their ends.
Inputs may be any that keep to these rules, and one draw needn't show every extreme that they name: `record_tile`: among the 256 records of one device, at most 48 name the same tile.
All inputs are finite; a program needn't handle non-finite values.
Results may differ from the reference program's by a relative error of at most 0.0003.
Values sent between devices are 32-bit elements; how exact they have to be, the bound alone decides.
A program may use at most 64 MiB of HBM per device.

```python
import math
import jax
import jax.numpy as jnp
import numpy as np
from jax import lax

CX = 16
NY = 64
NZ = 256
REC_DEV = 256
NT = 1536
STEPS = 6
SHOTS = 4
NX = 128
RECS = 2048
CAP = 48
GY = 80
N_SPACE = 8


def draw_adjoint_prev(key, part):
    own_key = jax.random.fold_in(key, 11)
    extent = (SHOTS, NY, NX, NZ)
    return jnp.clip(jax.random.normal(own_key, extent, jnp.float32), -6.0, 6.0)


def draw_adjoint_now(key, part):
    own_key = jax.random.fold_in(key, 12)
    extent = (SHOTS, NY, NX, NZ)
    return jnp.clip(jax.random.normal(own_key, extent, jnp.float32), -6.0, 6.0)


def set_ends(entries, key, low, largest):
    place = [jax.random.randint(jax.random.fold_in(key, axis), (), 0, length) for axis, length in enumerate(entries.shape)]
    widest = entries.shape.index(max(entries.shape))
    beside = place[:widest] + [(place[widest] + 1) % entries.shape[widest]] + place[widest + 1:]
    return entries.at[tuple(place)].set(low).at[tuple(beside)].set(largest)


def level_of(key, shape, split, low, high):
    def one(axis_at, blocks):
        draws = jax.random.uniform(jax.random.fold_in(jax.random.fold_in(key, 6), axis_at), (blocks,), jnp.float32, low / len(split), high / len(split))
        return jnp.repeat(jnp.exp(draws), shape[axis_at] // blocks).reshape((-1,) + (1,) * (len(shape) - axis_at - 1))

    factor_of = one(*split[0])
    for cut in split[1:]:
        factor_of = factor_of * one(*cut)
    return factor_of


def assign_block(rng, own, number, rows, amount, top, most, lean):
    ranking = jax.random.permutation(rng, amount)
    heavy_load, ordinary = load_shares(amount, rows * top, most, lean, True), load_shares(amount, rows * top, most, lean, False)
    places = jnp.arange(amount)

    def named(lengths, turn):
        used = int((lengths > 0).sum())
        fixed = max(1, used // 4)
        moved = fixed + (places - fixed + turn * (used - fixed)) % max(1, amount - fixed)
        return jnp.zeros((amount,), jnp.int32).at[ranking[jnp.where(places < fixed, places, moved)]].set(jnp.asarray(lengths, jnp.int32))

    lengths = jnp.where(number % 4 == 0, named(heavy_load, number // 4), named(ordinary, number - number // 4 - 1))
    mixed = jax.random.permutation(jax.random.fold_in(own, 3), amount)
    source_of, sink = mixed[0:amount // 2 * 2:2], mixed[1:amount // 2 * 2:2]
    room = jnp.minimum(lengths[source_of] - 1, most - lengths[sink]) // 2
    room = jnp.where((source_of == ranking[0]) | (sink == ranking[0]) | (lengths[sink] == 0), 0, jnp.maximum(room, 0))
    moved = jax.random.randint(jax.random.fold_in(own, 4), (amount // 2,), 0, 1 << 20) % (room + 1)
    lengths = lengths.at[source_of].add(-moved).at[sink].add(moved)
    members = jnp.searchsorted(jnp.cumsum(lengths), jnp.arange(rows * top), side="right").astype(jnp.int32)
    listing = members.reshape(top, rows).T
    listing = listing[jax.random.permutation(jax.random.fold_in(own, 1), rows)]
    turn = jax.random.randint(jax.random.fold_in(own, 2), (rows, 1), 0, top)
    return jnp.take_along_axis(listing, (jnp.arange(top)[None, :] + turn) % top, axis=1)


def load_shares(amount, total, limit, skew, full):
    portions = [(1 << 20) // math.isqrt(standing ** skew) + 1 for standing in range(1, amount + 1)]
    largest = limit if full else min(limit, max(-(-total // amount), total * portions[0] // sum(portions)))
    least = 1 if total - largest >= amount - 1 else 0
    counts, spare = [largest] + [least] * (amount - 1), total - largest - least * (amount - 1)
    while spare > 0:
        movable = [i for i in range(1, amount) if counts[i] < largest] or [i for i in range(1, amount) if counts[i] < limit]
        whole, left = sum([portions[i] for i in movable]), spare
        for i in movable:
            more = min(limit - counts[i], max(1, left * portions[i] // whole), spare)
            counts[i] = counts[i] + more
            spare = spare - more
    return np.array(counts)


def gaussian(stream_key, shape, deviation, bound, pieces=(), held_as=jnp.bfloat16):
    factor_of = level_of(stream_key, shape, pieces, -0.22, 0.18) if pieces else 1.0
    result = jax.random.normal(stream_key, shape, jnp.float32) * deviation * factor_of
    return jnp.minimum(jnp.maximum(result, -bound), bound).astype(held_as)


def setup_inputs(seed: int = 0) -> dict:
    arg_keys = jax.random.split(jax.random.key(seed), 10)
    residual = gaussian(arg_keys[0], (SHOTS, RECS, NT), 1.0, 6.0, ((0, 4), (1, 8)))
    record_tile_keys = jax.random.split(jax.random.fold_in(arg_keys[1], 1), SHOTS * RECS // REC_DEV)
    record_tile_turns = jax.random.permutation(jax.random.fold_in(arg_keys[1], 3), SHOTS * RECS // REC_DEV)
    record_tile = jax.vmap(lambda own, number: assign_block(jax.random.fold_in(arg_keys[1], 2), own, number, REC_DEV, N_SPACE, 1, CAP, 2))(record_tile_keys, record_tile_turns).reshape((SHOTS, RECS, 1))
    record_cell = set_ends(jax.random.randint(arg_keys[2], (SHOTS, RECS), 0, NY * CX), jax.random.fold_in(arg_keys[2], 1), 0, (NY * CX) - 1).astype(jnp.int32)
    time_filter = gaussian(arg_keys[3], (STEPS, NT), NT ** -0.5, 0.15625)
    offsets = set_ends(jax.random.randint(arg_keys[4], (SHOTS,), 0, NY // 4 + 1), jax.random.fold_in(arg_keys[4], 1), 0, (NY // 4 + 1) - 1).astype(jnp.int32)
    velocity = jnp.clip(0.05 + 0.14 * jax.random.uniform(arg_keys[5], (SHOTS, NY, NX, NZ), jnp.float32) ** level_of(arg_keys[5], (SHOTS, NY, NX, NZ), ((0, 4), (2, 8)), -0.2, 0.2), 0.05, 0.19)
    adjoint_prev = draw_adjoint_prev(jax.random.fold_in(arg_keys[9], 71), 0)
    adjoint_now = draw_adjoint_now(jax.random.fold_in(arg_keys[9], 71), 0)
    forward_accel = gaussian(arg_keys[8], (SHOTS, STEPS, NY, NX, NZ), 1.0, 6.0, ((0, 4), (3, 8)))
    return {"residual": residual, "record_tile": record_tile, "record_cell": record_cell, "time_filter": time_filter, "offsets": offsets, "velocity": velocity, "adjoint_prev": adjoint_prev, "adjoint_now": adjoint_now, "forward_accel": forward_accel}


STENCIL = (-205.0 / 72.0, 8.0 / 5.0, -1.0 / 5.0, 8.0 / 315.0, -1.0 / 560.0)


def laplace(padded):
    span_y = padded.shape[0] - 8
    span_x = padded.shape[1] - 8
    span_z = padded.shape[2] - 8

    def window(shift_y, shift_x, shift_z):
        return padded[4 + shift_y:4 + shift_y + span_y, 4 + shift_x:4 + shift_x + span_x, 4 + shift_z:4 + shift_z + span_z]

    summed = 3.0 * STENCIL[0] * window(0, 0, 0)
    for reach in range(1, 5):
        beside_all = window(reach, 0, 0) + window(-reach, 0, 0) + window(0, reach, 0) + window(0, -reach, 0) + window(0, 0, reach) + window(0, 0, -reach)
        summed = summed + STENCIL[reach] * beside_all
    return summed


def reference(residual, record_tile, record_cell, time_filter, offsets, velocity, adjoint_prev, adjoint_now, forward_accel):
    gradient = jnp.zeros((GY, NX, NZ), jnp.float32)
    finals = []
    zero_index = jnp.zeros((), jnp.int32)
    for shot in range(SHOTS):
        values = jnp.dot(residual[shot], time_filter.T, preferred_element_type=jnp.float32)
        cell_ids = record_cell[shot]
        column = record_tile[shot, :, 0] * CX + cell_ids % CX
        surface_index = (cell_ids // CX) * NX + column
        source = jax.ops.segment_sum(values, surface_index, num_segments=NY * NX)
        source = source.T.reshape(STEPS, NY, NX)
        speed_sq = velocity[shot]
        previous = adjoint_prev[shot]
        current = adjoint_now[shot]
        imaging = jnp.zeros_like(current)
        for moment in range(STEPS):
            advanced = 2.0 * current - previous + speed_sq * laplace(jnp.pad(current, 4))
            advanced = advanced.at[:, :, 0].add(source[moment])
            imaging = imaging + forward_accel[shot, moment].astype(jnp.float32) * advanced
            previous, current = current, advanced
        placed = lax.dynamic_update_slice(jnp.zeros((GY, NX, NZ), jnp.float32), imaging, (offsets[shot].astype(jnp.int32), zero_index, zero_index))
        gradient = gradient + placed
        finals.append(current)
    return gradient, jnp.stack(finals)
```

```python
import functools

import jax
import jax.numpy as jnp
import numpy as np
from jax import lax
from jax.experimental import pallas as pl
from jax.experimental.pallas import tpu as pltpu
from jax.sharding import PartitionSpec as P

STENCIL = (-205.0 / 72.0, 8.0 / 5.0, -1.0 / 5.0, 8.0 / 315.0, -1.0 / 560.0)
MESH = pl.DeviceIdType.MESH
F32 = jnp.float32
BF16 = jnp.bfloat16
CX = 16
CHUNK_Y = 16
ROWS = CHUNK_Y * CX
EDGE = CHUNK_Y * 4
PAD = 64


def pieces(matrix):
    high = np.asarray(matrix, np.float32).astype(jnp.bfloat16)
    low = (matrix - high.astype(np.float64)).astype(np.float32).astype(jnp.bfloat16)
    return high, low


def coefficient(distance):
    distance = abs(distance)
    return STENCIL[distance] if 1 <= distance <= 4 else 0.0


def matrices(depth):
    along_z = np.zeros((depth, depth))
    for i in range(depth):
        along_z[i, i] = 3.0 * STENCIL[0]
        for j in range(max(0, i - 4), min(depth, i + 5)):
            if i != j:
                along_z[j, i] = coefficient(i - j)
    across = np.zeros((8 * CX, 16 * CX))
    for y in range(8):
        for x in range(CX):
            for other in range(16):
                across[y * CX + x, other * CX + x] += coefficient(other - 4 - y)
            for other in range(CX):
                across[y * CX + x, (y + 4) * CX + other] += coefficient(other - x)
    rim = np.zeros((ROWS, 2 * EDGE))
    for y in range(CHUNK_Y):
        for x in range(CX):
            for j in range(4):
                rim[y * CX + x, y * 4 + j] = coefficient(x + 4 - j)
                rim[y * CX + x, EDGE + y * 4 + j] = coefficient(16 + j - x)
    z_high, z_low = pieces(along_z)
    a_high, a_low = pieces(across)
    r_high, r_low = pieces(rim)
    return (
        z_high,
        z_low,
        np.concatenate([a_high, a_low], axis=0),
        np.concatenate([r_high, r_high], axis=1),
        r_low,
    )


def split(value):
    high = value.astype(BF16)
    low = (value - high.astype(F32)).astype(BF16)
    return high, low


def dot(a, b):
    return jnp.dot(a, b, preferred_element_type=F32)


def dot_nt(a, b):
    return lax.dot_general(a, b, (((1,), (1,)), ((), ())), preferred_element_type=F32)


def kernel(
    spaces,
    shots,
    steps,
    residual,
    codes,
    time_filter,
    offsets,
    z_high,
    z_low,
    across,
    rim_high,
    rim_low,
    now_hbm,
    previous_hbm,
    velocity_hbm,
    forward_hbm,
    gradient,
    last_hbm,
    q,
    high,
    low,
    speed,
    forward,
    image,
    source,
    gathered,
    halo_out,
    halo_in,
    stack_out,
    stack_in,
    local_sem,
    gather_send,
    gather_recv,
    halo_send,
    halo_recv,
    stack_send,
    stack_recv,
):
    cells = q.shape[1]
    chunks = cells // ROWS
    depth = q.shape[2]
    band = gradient.shape[0]
    lead = cells // CX // 4
    shot = lax.axis_index("shot")
    me = lax.axis_index("space")

    loads = [
        pltpu.make_async_copy(now_hbm, q.at[0], local_sem.at[0]),
        pltpu.make_async_copy(previous_hbm, q.at[1], local_sem.at[1]),
        pltpu.make_async_copy(velocity_hbm, speed, local_sem.at[2]),
        pltpu.make_async_copy(forward_hbm, forward, local_sem.at[3]),
    ]
    for load in loads:
        load.start()

    barrier = pltpu.get_barrier_semaphore()
    for d in range(1, spaces):
        pl.semaphore_signal(
            barrier, inc=1, device_id=(shot, lax.rem(me + d, spaces)), device_id_type=MESH
        )
    for d in range(1, shots):
        pl.semaphore_signal(
            barrier, inc=1, device_id=(lax.rem(shot + d, shots), me), device_id_type=MESH
        )

    gathered[me, 0:8, :] = jnp.zeros((8, gathered.shape[2]), F32)
    gathered[me, 0:steps, :] = dot_nt(time_filter[...], residual[...])
    gathered[me, 6:7, :] = codes[...]

    for slot in range(2):
        for piece in (high, low):
            piece[slot, 0:PAD, :] = jnp.zeros((PAD, depth), BF16)
            piece[slot, PAD + cells :, :] = jnp.zeros((PAD, depth), BF16)
    image[...] = jnp.zeros(image.shape, F32)

    has_left = me > 0
    has_right = me < spaces - 1

    @pl.when(jnp.logical_not(has_left))
    def _():
        halo_in[:, 0] = jnp.zeros((2,) + halo_in.shape[2:], F32)

    @pl.when(jnp.logical_not(has_right))
    def _():
        halo_in[:, 1] = jnp.zeros((2,) + halo_in.shape[2:], F32)

    pl.semaphore_wait(barrier, spaces - 1 + shots - 1)

    def gather_copy(d):
        return pltpu.make_async_remote_copy(
            src_ref=gathered.at[me],
            dst_ref=gathered.at[me],
            send_sem=gather_send.at[d - 1],
            recv_sem=gather_recv.at[d - 1],
            device_id=(shot, lax.rem(me + d, spaces)),
            device_id_type=MESH,
        )

    def gather_arrival(d):
        owner = lax.rem(me + spaces - d, spaces)
        return pltpu.make_async_remote_copy(
            src_ref=gathered.at[owner],
            dst_ref=gathered.at[owner],
            send_sem=gather_send.at[d - 1],
            recv_sem=gather_recv.at[d - 1],
            device_id=(shot, lax.rem(me + d, spaces)),
            device_id_type=MESH,
        )

    def halo_copy(slot, side, c):
        target = me - 1 if side == 0 else me + 1
        rows = pl.ds(c * EDGE, EDGE)
        return pltpu.make_async_remote_copy(
            src_ref=halo_out.at[slot, side, rows],
            dst_ref=halo_in.at[slot, 1 - side, rows],
            send_sem=halo_send.at[slot, side, c],
            recv_sem=halo_recv.at[slot, 1 - side, c],
            device_id=(shot, target),
            device_id_type=MESH,
        )

    def halo_arrival(slot, side, c):
        target = me - 1 if side == 0 else me + 1
        rows = pl.ds(c * EDGE, EDGE)
        return pltpu.make_async_remote_copy(
            src_ref=halo_out.at[slot, side, rows],
            dst_ref=halo_in.at[slot, side, rows],
            send_sem=halo_send.at[slot, side, c],
            recv_sem=halo_recv.at[slot, side, c],
            device_id=(shot, target),
            device_id_type=MESH,
        )

    first_half = lax.broadcasted_iota(jnp.int32, (8, depth), 0) < 4

    def publish_edges(slot, c, value):
        for pair in range(CHUNK_Y // 2):
            base = pair * 2 * CX
            low_a = value[base : base + 8]
            high_a = value[base + 8 : base + 16]
            low_b = value[base + 16 : base + 24]
            high_b = value[base + 24 : base + 32]
            at = pl.ds(c * EDGE + pair * 8, 8)
            halo_out[slot, 0, at, :] = jnp.where(first_half, low_a, pltpu.roll(low_b, 4, 0))
            halo_out[slot, 1, at, :] = jnp.where(first_half, pltpu.roll(high_a, 4, 0), high_b)

        @pl.when(has_left)
        def _():
            halo_copy(slot, 0, c).start()

        @pl.when(has_right)
        def _():
            halo_copy(slot, 1, c).start()

    def wait_edges_sent(slot, c):
        @pl.when(has_left)
        def _():
            halo_copy(slot, 0, c).wait_send()

        @pl.when(has_right)
        def _():
            halo_copy(slot, 1, c).wait_send()

    def publish_pieces(slot, c, value):
        value_high, value_low = split(value)
        high[slot, pl.ds(PAD + c * ROWS, ROWS), :] = value_high
        low[slot, pl.ds(PAD + c * ROWS, ROWS), :] = value_low

    for d in range(1, spaces):
        gather_copy(d).start()
    loads[0].wait()
    for c in range(chunks):
        publish_edges(0, c, q[0, pl.ds(c * ROWS, ROWS), :])
    for c in range(chunks):
        publish_pieces(0, c, q[0, pl.ds(c * ROWS, ROWS), :])

    for d in range(1, spaces):
        gather_arrival(d).wait_recv()
    first_cell = (me * cells).astype(F32)

    def add_block(j, totals):
        block = gathered[j]
        block_high = block.astype(BF16).astype(F32)
        stacked = jnp.concatenate(
            [block_high, block - block_high, jnp.zeros((112, block.shape[1]), F32)], axis=0
        ).astype(BF16)
        wanted = block[6:7, :] - first_cell
        for c in range(chunks):
            cell = (lax.broadcasted_iota(jnp.int32, (ROWS, block.shape[1]), 0) + c * ROWS).astype(F32)
            hot = jnp.where(wanted == cell, 1.0, 0.0).astype(BF16)
            source[pl.ds(c * ROWS, ROWS), :] += dot_nt(hot, stacked)
        return totals

    source[...] = jnp.zeros(source.shape, F32)
    lax.fori_loop(0, spaces, add_block, 0)
    source[...] = source[...] + pltpu.roll(source[...], 120, 1)

    for load in loads[1:]:
        load.wait()

    first_lane = lax.broadcasted_iota(jnp.int32, (ROWS, 128), 1) == 0

    def step(k, carry):
        slot = lax.rem(k, 2)
        other = 1 - slot
        for c in range(chunks):
            rows = pl.ds(c * ROWS, ROWS)
            mid_high = high[slot, pl.ds(PAD + c * ROWS, ROWS), :]
            mid_low = low[slot, pl.ds(PAD + c * ROWS, ROWS), :]
            spread = dot(mid_high, z_high[...]) + dot(mid_high, z_low[...])
            spread = spread + dot(mid_low, z_high[...])
            parts = []
            for sub in range(2):
                window = pl.ds((2 * c + sub) * 128, 256)
                both = dot(across[...], high[slot, window, :])
                parts.append(both[:128] + both[128:] + dot(across[0:128], low[slot, window, :]))
            spread = spread + jnp.concatenate(parts, axis=0)

            @pl.when(has_left)
            def _():
                halo_arrival(slot, 0, c).wait_recv()

            @pl.when(has_right)
            def _():
                halo_arrival(slot, 1, c).wait_recv()

            at = pl.ds(c * EDGE, EDGE)
            rim = jnp.concatenate([halo_in[slot, 0, at, :], halo_in[slot, 1, at, :]], axis=0)
            rim_h, rim_l = split(rim)
            spread = spread + dot(rim_high[...], jnp.concatenate([rim_h, rim_l], axis=0))
            spread = spread + dot(rim_low[...], rim_h)

            value = 2.0 * q[slot, rows, :] - q[other, rows, :] + speed[rows, :] * spread
            added = source[rows, :]
            first = value[:, :128] + jnp.where(first_lane, added, 0.0)
            source[rows, :] = pltpu.roll(added, 127, 1)
            value = jnp.concatenate([first, value[:, 128:]], axis=1)
            q[other, rows, :] = value

            @pl.when(k < steps - 1)
            def _():
                @pl.when(k >= 1)
                def _():
                    wait_edges_sent(other, c)

                publish_edges(other, c, value)
                publish_pieces(other, c, value)

            inside = pl.ds(lead + c * CHUNK_Y, CHUNK_Y)
            product = forward[k, rows, :].astype(F32) * value
            image[inside] += product.reshape(CHUNK_Y, CX, depth)
        return carry

    lax.fori_loop(0, steps, step, 0)
    result = pltpu.make_async_copy(q.at[steps % 2], last_hbm, local_sem.at[0])
    result.start()

    moved = offsets[0]
    band_y = band // CX

    def shift_into(place, owner):
        for y in range(band_y):
            place[pl.ds(y * CX, CX), :] = image[owner * band_y + y - moved + lead]

    copies = []
    for d in range(1, shots):
        target = lax.rem(shot + d, shots)
        shift_into(stack_out.at[d - 1], target)
        copy = pltpu.make_async_remote_copy(
            src_ref=stack_out.at[d - 1],
            dst_ref=stack_in.at[d - 1],
            send_sem=stack_send.at[d - 1],
            recv_sem=stack_recv.at[d - 1],
            device_id=(target, me),
            device_id_type=MESH,
        )
        copy.start()
        copies.append(copy)
    shift_into(gradient, shot)
    for d in range(1, spaces):
        gather_copy(d).wait_send()
    for slot in range(2):
        for c in range(chunks):
            wait_edges_sent(slot, c)
    for d, copy in enumerate(copies):
        copy.wait_recv()
        gradient[...] += stack_in[d]
    for copy in copies:
        copy.wait_send()
    result.wait()


def local(
    spaces,
    shots,
    residual,
    record_tile,
    record_cell,
    time_filter,
    offsets,
    velocity,
    adjoint_prev,
    adjoint_now,
    forward_accel,
):
    _, ny, cx, depth = velocity.shape
    steps = forward_accel.shape[1]
    cells = ny * cx
    records = residual.shape[1]
    grid_y = ny + ny // 4
    band = grid_y // shots * cx
    chunks = cells // ROWS
    codes = (record_tile[0, :, 0] * cells + record_cell[0]).astype(F32)[None]
    constants = [jnp.asarray(matrix) for matrix in matrices(depth)]
    vmem = pl.BlockSpec(memory_space=pltpu.VMEM)
    anywhere = pl.BlockSpec(memory_space=pl.ANY)
    gradient, last = pl.pallas_call(
        functools.partial(kernel, spaces, shots, steps),
        out_shape=(
            jax.ShapeDtypeStruct((band, depth), F32),
            jax.ShapeDtypeStruct((cells, depth), F32),
        ),
        in_specs=[vmem] * 3
        + [pl.BlockSpec(memory_space=pltpu.SMEM)]
        + [vmem] * 5
        + [anywhere] * 4,
        out_specs=(vmem, anywhere),
        scratch_shapes=[
            pltpu.VMEM((2, cells, depth), F32),
            pltpu.VMEM((2, cells + 2 * PAD, depth), BF16),
            pltpu.VMEM((2, cells + 2 * PAD, depth), BF16),
            pltpu.VMEM((cells, depth), F32),
            pltpu.VMEM((steps, cells, depth), BF16),
            pltpu.VMEM((ny + 2 * (ny // 4), cx, depth), F32),
            pltpu.VMEM((cells, 128), F32),
            pltpu.VMEM((spaces, 8, records), F32),
            pltpu.VMEM((2, 2, chunks * EDGE, depth), F32),
            pltpu.VMEM((2, 2, chunks * EDGE, depth), F32),
            pltpu.VMEM((shots - 1, band, depth), F32),
            pltpu.VMEM((shots - 1, band, depth), F32),
            pltpu.SemaphoreType.DMA((4,)),
            pltpu.SemaphoreType.DMA((spaces - 1,)),
            pltpu.SemaphoreType.DMA((spaces - 1,)),
            pltpu.SemaphoreType.DMA((2, 2, chunks)),
            pltpu.SemaphoreType.DMA((2, 2, chunks)),
            pltpu.SemaphoreType.DMA((shots - 1,)),
            pltpu.SemaphoreType.DMA((shots - 1,)),
        ],
        compiler_params=pltpu.CompilerParams(
            collective_id=0, has_side_effects=True, vmem_limit_bytes=44 * 1024 * 1024
        ),
        cost_estimate=pl.CostEstimate(flops=6 * 10**9, bytes_accessed=8 * 10**6, transcendentals=0),
    )(
        residual[0],
        codes,
        time_filter,
        offsets,
        *constants,
        adjoint_now.reshape(cells, depth),
        adjoint_prev.reshape(cells, depth),
        velocity.reshape(cells, depth),
        forward_accel.reshape(steps, cells, depth),
    )
    return gradient.reshape(grid_y // shots, cx, depth), last.reshape(1, ny, cx, depth)


def solution(mesh):
    in_specs = (
        P("shot", "space", None),
        P("shot", "space", None),
        P("shot", "space"),
        P(),
        P("shot"),
        P("shot", None, "space", None),
        P("shot", None, "space", None),
        P("shot", None, "space", None),
        P("shot", None, None, "space", None),
    )
    out_specs = (P("shot", "space", None), P("shot", None, "space", None))
    body = functools.partial(local, mesh.shape["space"], mesh.shape["shot"])
    return jax.shard_map(body, mesh=mesh, in_specs=in_specs, out_specs=out_specs, check_vma=False)
```

```python
import functools

import jax
import jax.numpy as jnp
import numpy as np
from jax import lax
from jax.experimental import pallas as pl
from jax.experimental.pallas import tpu as pltpu
from jax.sharding import PartitionSpec as P

STENCIL = (-205.0 / 72.0, 8.0 / 5.0, -1.0 / 5.0, 8.0 / 315.0, -1.0 / 560.0)
MESH = pl.DeviceIdType.MESH
F32 = jnp.float32
BF16 = jnp.bfloat16
CX = 16
CHUNK_Y = 16
ROWS = CHUNK_Y * CX
EDGE = CHUNK_Y * 4
PAD = 64


def pieces(matrix):
    high = np.asarray(matrix, np.float32).astype(jnp.bfloat16)
    low = (matrix - high.astype(np.float64)).astype(np.float32).astype(jnp.bfloat16)
    return high, low


def coefficient(distance):
    distance = abs(distance)
    return STENCIL[distance] if 1 <= distance <= 4 else 0.0


def matrices(depth):
    along_z = np.zeros((depth, depth))
    for i in range(depth):
        along_z[i, i] = 3.0 * STENCIL[0]
        for j in range(max(0, i - 4), min(depth, i + 5)):
            if i != j:
                along_z[j, i] = coefficient(i - j)
    across = np.zeros((8 * CX, 16 * CX))
    for y in range(8):
        for x in range(CX):
            for other in range(16):
                across[y * CX + x, other * CX + x] += coefficient(other - 4 - y)
            for other in range(CX):
                across[y * CX + x, (y + 4) * CX + other] += coefficient(other - x)
    rim = np.zeros((ROWS, 2 * EDGE))
    for y in range(CHUNK_Y):
        for x in range(CX):
            for j in range(4):
                rim[y * CX + x, y * 4 + j] = coefficient(x + 4 - j)
                rim[y * CX + x, EDGE + y * 4 + j] = coefficient(16 + j - x)
    z_high, z_low = pieces(along_z)
    a_high, a_low = pieces(across)
    r_high, r_low = pieces(rim)
    return (
        z_high,
        z_low,
        np.concatenate([a_high, a_low], axis=0),
        np.concatenate([r_high, r_high], axis=1),
        r_low,
    )


def split(value):
    high = value.astype(BF16)
    low = (value - high.astype(F32)).astype(BF16)
    return high, low


def dot(a, b):
    return jnp.dot(a, b, preferred_element_type=F32)


def dot_nt(a, b):
    return lax.dot_general(a, b, (((1,), (1,)), ((), ())), preferred_element_type=F32)


def kernel(
    spaces,
    shots,
    steps,
    residual_hbm,
    codes,
    filter_hbm,
    offsets,
    z_high_hbm,
    z_low_hbm,
    across_hbm,
    rim_high_hbm,
    rim_low_hbm,
    now_hbm,
    previous_hbm,
    velocity_hbm,
    forward_hbm,
    gradient,
    last_hbm,
    residual,
    time_filter,
    z_high,
    z_low,
    across,
    rim_high,
    rim_low,
    q,
    high,
    low,
    speed,
    forward,
    image,
    source,
    gathered,
    halo_out,
    halo_in,
    stack_out,
    stack_in,
    local_sem,
    gather_send,
    gather_recv,
    halo_send,
    halo_recv,
    stack_send,
    stack_recv,
):
    cells = q.shape[1]
    chunks = cells // ROWS
    depth = q.shape[2]
    band = gradient.shape[0]
    lead = cells // CX // 4
    shot = lax.axis_index("shot")
    me = lax.axis_index("space")

    pairs = (
        (now_hbm, q.at[0]),
        (residual_hbm, residual),
        (filter_hbm, time_filter),
        (z_high_hbm, z_high),
        (z_low_hbm, z_low),
        (across_hbm, across),
        (rim_high_hbm, rim_high),
        (rim_low_hbm, rim_low),
        (previous_hbm, q.at[1]),
        (velocity_hbm, speed),
        (forward_hbm, forward),
    )
    loads = [
        pltpu.make_async_copy(there, here, local_sem.at[i]) for i, (there, here) in enumerate(pairs)
    ]
    for load in loads:
        load.start()

    barrier = pltpu.get_barrier_semaphore()
    for d in range(1, spaces):
        pl.semaphore_signal(
            barrier, inc=1, device_id=(shot, lax.rem(me + d, spaces)), device_id_type=MESH
        )
    for d in range(1, shots):
        pl.semaphore_signal(
            barrier, inc=1, device_id=(lax.rem(shot + d, shots), me), device_id_type=MESH
        )

    for slot in range(2):
        for piece in (high, low):
            piece[slot, 0:PAD, :] = jnp.zeros((PAD, depth), BF16)
            piece[slot, PAD + cells :, :] = jnp.zeros((PAD, depth), BF16)
    image[...] = jnp.zeros(image.shape, F32)

    has_left = me > 0
    has_right = me < spaces - 1

    @pl.when(jnp.logical_not(has_left))
    def _():
        halo_in[:, 0] = jnp.zeros((2,) + halo_in.shape[2:], F32)

    @pl.when(jnp.logical_not(has_right))
    def _():
        halo_in[:, 1] = jnp.zeros((2,) + halo_in.shape[2:], F32)

    pl.semaphore_wait(barrier, spaces - 1 + shots - 1)

    def gather_copy(d):
        return pltpu.make_async_remote_copy(
            src_ref=gathered.at[me],
            dst_ref=gathered.at[me],
            send_sem=gather_send.at[d - 1],
            recv_sem=gather_recv.at[d - 1],
            device_id=(shot, lax.rem(me + d, spaces)),
            device_id_type=MESH,
        )

    def gather_arrival(d):
        owner = lax.rem(me + spaces - d, spaces)
        return pltpu.make_async_remote_copy(
            src_ref=gathered.at[owner],
            dst_ref=gathered.at[owner],
            send_sem=gather_send.at[d - 1],
            recv_sem=gather_recv.at[d - 1],
            device_id=(shot, lax.rem(me + d, spaces)),
            device_id_type=MESH,
        )

    def halo_copy(slot, side, c):
        target = me - 1 if side == 0 else me + 1
        rows = pl.ds(c * EDGE, EDGE)
        return pltpu.make_async_remote_copy(
            src_ref=halo_out.at[slot, side, rows],
            dst_ref=halo_in.at[slot, 1 - side, rows],
            send_sem=halo_send.at[slot, side, c],
            recv_sem=halo_recv.at[slot, 1 - side, c],
            device_id=(shot, target),
            device_id_type=MESH,
        )

    def halo_arrival(slot, side, c):
        target = me - 1 if side == 0 else me + 1
        rows = pl.ds(c * EDGE, EDGE)
        return pltpu.make_async_remote_copy(
            src_ref=halo_out.at[slot, side, rows],
            dst_ref=halo_in.at[slot, side, rows],
            send_sem=halo_send.at[slot, side, c],
            recv_sem=halo_recv.at[slot, side, c],
            device_id=(shot, target),
            device_id_type=MESH,
        )

    first_half = lax.broadcasted_iota(jnp.int32, (8, depth), 0) < 4

    def publish_edges(slot, c, value):
        for pair in range(CHUNK_Y // 2):
            base = pair * 2 * CX
            low_a = value[base : base + 8]
            high_a = value[base + 8 : base + 16]
            low_b = value[base + 16 : base + 24]
            high_b = value[base + 24 : base + 32]
            at = pl.ds(c * EDGE + pair * 8, 8)
            halo_out[slot, 0, at, :] = jnp.where(first_half, low_a, pltpu.roll(low_b, 4, 0))
            halo_out[slot, 1, at, :] = jnp.where(first_half, pltpu.roll(high_a, 4, 0), high_b)

        @pl.when(has_left)
        def _():
            halo_copy(slot, 0, c).start()

        @pl.when(has_right)
        def _():
            halo_copy(slot, 1, c).start()

    def wait_edges_sent(slot, c):
        @pl.when(has_left)
        def _():
            halo_copy(slot, 0, c).wait_send()

        @pl.when(has_right)
        def _():
            halo_copy(slot, 1, c).wait_send()

    def publish_pieces(slot, c, value):
        value_high, value_low = split(value)
        high[slot, pl.ds(PAD + c * ROWS, ROWS), :] = value_high
        low[slot, pl.ds(PAD + c * ROWS, ROWS), :] = value_low

    loads[0].wait()
    for c in range(chunks):
        publish_edges(0, c, q[0, pl.ds(c * ROWS, ROWS), :])
    loads[1].wait()
    loads[2].wait()
    gathered[me, 0:8, :] = jnp.zeros((8, gathered.shape[2]), F32)
    gathered[me, 0:steps, :] = dot_nt(time_filter[...], residual[...])
    gathered[me, 6:7, :] = codes[...]
    for d in range(1, spaces):
        gather_copy(d).start()
    for c in range(chunks):
        publish_pieces(0, c, q[0, pl.ds(c * ROWS, ROWS), :])

    for d in range(1, spaces):
        gather_arrival(d).wait_recv()
    first_cell = (me * cells).astype(F32)

    def add_block(j, totals):
        block = gathered[j]
        block_high = block.astype(BF16).astype(F32)
        stacked = jnp.concatenate(
            [block_high, block - block_high, jnp.zeros((112, block.shape[1]), F32)], axis=0
        ).astype(BF16)
        wanted = block[6:7, :] - first_cell
        for c in range(chunks):
            cell = (lax.broadcasted_iota(jnp.int32, (ROWS, block.shape[1]), 0) + c * ROWS).astype(F32)
            hot = jnp.where(wanted == cell, 1.0, 0.0).astype(BF16)
            source[pl.ds(c * ROWS, ROWS), :] += dot_nt(hot, stacked)
        return totals

    source[...] = jnp.zeros(source.shape, F32)
    lax.fori_loop(0, spaces, add_block, 0)
    source[...] = source[...] + pltpu.roll(source[...], 120, 1)

    for load in loads[3:]:
        load.wait()

    first_lane = lax.broadcasted_iota(jnp.int32, (ROWS, 128), 1) == 0

    def step(k, carry):
        slot = lax.rem(k, 2)
        other = 1 - slot
        for c in range(chunks):
            rows = pl.ds(c * ROWS, ROWS)
            mid_high = high[slot, pl.ds(PAD + c * ROWS, ROWS), :]
            mid_low = low[slot, pl.ds(PAD + c * ROWS, ROWS), :]
            spread = dot(mid_high, z_high[...]) + dot(mid_high, z_low[...])
            spread = spread + dot(mid_low, z_high[...])
            parts = []
            for sub in range(2):
                window = pl.ds((2 * c + sub) * 128, 256)
                both = dot(across[...], high[slot, window, :])
                parts.append(both[:128] + both[128:] + dot(across[0:128], low[slot, window, :]))
            spread = spread + jnp.concatenate(parts, axis=0)

            @pl.when(has_left)
            def _():
                halo_arrival(slot, 0, c).wait_recv()

            @pl.when(has_right)
            def _():
                halo_arrival(slot, 1, c).wait_recv()

            at = pl.ds(c * EDGE, EDGE)
            rim = jnp.concatenate([halo_in[slot, 0, at, :], halo_in[slot, 1, at, :]], axis=0)
            rim_h, rim_l = split(rim)
            spread = spread + dot(rim_high[...], jnp.concatenate([rim_h, rim_l], axis=0))
            spread = spread + dot(rim_low[...], rim_h)

            value = 2.0 * q[slot, rows, :] - q[other, rows, :] + speed[rows, :] * spread
            added = source[rows, :]
            first = value[:, :128] + jnp.where(first_lane, added, 0.0)
            source[rows, :] = pltpu.roll(added, 127, 1)
            value = jnp.concatenate([first, value[:, 128:]], axis=1)
            q[other, rows, :] = value

            @pl.when(k < steps - 1)
            def _():
                @pl.when(k >= 1)
                def _():
                    wait_edges_sent(other, c)

                publish_edges(other, c, value)
                publish_pieces(other, c, value)

            inside = pl.ds(lead + c * CHUNK_Y, CHUNK_Y)
            product = forward[k, rows, :].astype(F32) * value
            image[inside] += product.reshape(CHUNK_Y, CX, depth)
        return carry

    lax.fori_loop(0, steps, step, 0)
    result = pltpu.make_async_copy(q.at[steps % 2], last_hbm, local_sem.at[0])
    result.start()

    moved = offsets[0]
    band_y = band // CX

    def shift_into(place, owner):
        for y in range(band_y):
            place[pl.ds(y * CX, CX), :] = image[owner * band_y + y - moved + lead]

    copies = []
    for d in range(1, shots):
        target = lax.rem(shot + d, shots)
        shift_into(stack_out.at[d - 1], target)
        copy = pltpu.make_async_remote_copy(
            src_ref=stack_out.at[d - 1],
            dst_ref=stack_in.at[d - 1],
            send_sem=stack_send.at[d - 1],
            recv_sem=stack_recv.at[d - 1],
            device_id=(target, me),
            device_id_type=MESH,
        )
        copy.start()
        copies.append(copy)
    shift_into(gradient, shot)
    for d in range(1, spaces):
        gather_copy(d).wait_send()
    for slot in range(2):
        for c in range(chunks):
            wait_edges_sent(slot, c)
    for d, copy in enumerate(copies):
        copy.wait_recv()
        gradient[...] += stack_in[d]
    for copy in copies:
        copy.wait_send()
    result.wait()


def local(
    spaces,
    shots,
    residual,
    record_tile,
    record_cell,
    time_filter,
    offsets,
    velocity,
    adjoint_prev,
    adjoint_now,
    forward_accel,
):
    _, ny, cx, depth = velocity.shape
    steps = forward_accel.shape[1]
    cells = ny * cx
    records = residual.shape[1]
    grid_y = ny + ny // 4
    band = grid_y // shots * cx
    chunks = cells // ROWS
    codes = (record_tile[0, :, 0] * cells + record_cell[0]).astype(F32)[None]
    constants = [jnp.asarray(matrix) for matrix in matrices(depth)]
    vmem = pl.BlockSpec(memory_space=pltpu.VMEM)
    there = pl.BlockSpec(memory_space=pltpu.HBM)
    gradient, last = pl.pallas_call(
        functools.partial(kernel, spaces, shots, steps),
        out_shape=(
            jax.ShapeDtypeStruct((band, depth), F32),
            jax.ShapeDtypeStruct((cells, depth), F32),
        ),
        in_specs=[there, vmem, there, pl.BlockSpec(memory_space=pltpu.SMEM)] + [there] * 9,
        out_specs=(vmem, pl.BlockSpec(memory_space=pl.ANY)),
        scratch_shapes=[
            pltpu.VMEM((records, residual.shape[2]), BF16),
            pltpu.VMEM(time_filter.shape, BF16),
            *[pltpu.VMEM(matrix.shape, BF16) for matrix in constants],
            pltpu.VMEM((2, cells, depth), F32),
            pltpu.VMEM((2, cells + 2 * PAD, depth), BF16),
            pltpu.VMEM((2, cells + 2 * PAD, depth), BF16),
            pltpu.VMEM((cells, depth), F32),
            pltpu.VMEM((steps, cells, depth), BF16),
            pltpu.VMEM((ny + 2 * (ny // 4), cx, depth), F32),
            pltpu.VMEM((cells, 128), F32),
            pltpu.VMEM((spaces, 8, records), F32),
            pltpu.VMEM((2, 2, chunks * EDGE, depth), F32),
            pltpu.VMEM((2, 2, chunks * EDGE, depth), F32),
            pltpu.VMEM((shots - 1, band, depth), F32),
            pltpu.VMEM((shots - 1, band, depth), F32),
            pltpu.SemaphoreType.DMA((11,)),
            pltpu.SemaphoreType.DMA((spaces - 1,)),
            pltpu.SemaphoreType.DMA((spaces - 1,)),
            pltpu.SemaphoreType.DMA((2, 2, chunks)),
            pltpu.SemaphoreType.DMA((2, 2, chunks)),
            pltpu.SemaphoreType.DMA((shots - 1,)),
            pltpu.SemaphoreType.DMA((shots - 1,)),
        ],
        compiler_params=pltpu.CompilerParams(
            collective_id=0, has_side_effects=True, vmem_limit_bytes=44 * 1024 * 1024
        ),
        cost_estimate=pl.CostEstimate(flops=6 * 10**9, bytes_accessed=8 * 10**6, transcendentals=0),
    )(
        residual[0],
        codes,
        time_filter,
        offsets,
        *constants,
        adjoint_now.reshape(cells, depth),
        adjoint_prev.reshape(cells, depth),
        velocity.reshape(cells, depth),
        forward_accel.reshape(steps, cells, depth),
    )
    return gradient.reshape(grid_y // shots, cx, depth), last.reshape(1, ny, cx, depth)


def solution(mesh):
    in_specs = (
        P("shot", "space", None),
        P("shot", "space", None),
        P("shot", "space"),
        P(),
        P("shot"),
        P("shot", None, "space", None),
        P("shot", None, "space", None),
        P("shot", None, "space", None),
        P("shot", None, None, "space", None),
    )
    out_specs = (P("shot", "space", None), P("shot", None, "space", None))
    body = functools.partial(local, mesh.shape["space"], mesh.shape["shot"])
    return jax.shard_map(body, mesh=mesh, in_specs=in_specs, out_specs=out_specs, check_vma=False)
```

```python
import functools

import jax
import jax.numpy as jnp
import numpy as np
from jax import lax
from jax.experimental import pallas as pl
from jax.experimental.pallas import tpu as pltpu
from jax.sharding import PartitionSpec as P

STENCIL = (-205.0 / 72.0, 8.0 / 5.0, -1.0 / 5.0, 8.0 / 315.0, -1.0 / 560.0)
MESH = pl.DeviceIdType.MESH
F32 = jnp.float32
BF16 = jnp.bfloat16
CX = 16
CHUNK_Y = 16
ROWS = CHUNK_Y * CX
EDGE = CHUNK_Y * 4
PAD = 64


def pieces(matrix):
    high = np.asarray(matrix, np.float32).astype(jnp.bfloat16)
    low = (matrix - high.astype(np.float64)).astype(np.float32).astype(jnp.bfloat16)
    return high, low


def coefficient(distance):
    distance = abs(distance)
    return STENCIL[distance] if 1 <= distance <= 4 else 0.0


def matrices(depth):
    along_z = np.zeros((depth, depth))
    for i in range(depth):
        along_z[i, i] = 3.0 * STENCIL[0]
        for j in range(max(0, i - 4), min(depth, i + 5)):
            if i != j:
                along_z[j, i] = coefficient(i - j)
    across = np.zeros((8 * CX, 16 * CX))
    for y in range(8):
        for x in range(CX):
            for other in range(16):
                across[y * CX + x, other * CX + x] += coefficient(other - 4 - y)
            for other in range(CX):
                across[y * CX + x, (y + 4) * CX + other] += coefficient(other - x)
    rim = np.zeros((ROWS, 2 * EDGE))
    for y in range(CHUNK_Y):
        for x in range(CX):
            for j in range(4):
                rim[y * CX + x, y * 4 + j] = coefficient(x + 4 - j)
                rim[y * CX + x, EDGE + y * 4 + j] = coefficient(16 + j - x)
    z_high, z_low = pieces(along_z)
    a_high, a_low = pieces(across)
    r_high, r_low = pieces(rim)
    return (
        z_high,
        z_low,
        np.concatenate([a_high, a_low], axis=0),
        np.concatenate([r_high, r_high], axis=1),
        r_low,
    )


def split(value):
    high = value.astype(BF16)
    low = (value - high.astype(F32)).astype(BF16)
    return high, low


def dot(a, b):
    return jnp.dot(a, b, preferred_element_type=F32)


def dot_nt(a, b):
    return lax.dot_general(a, b, (((1,), (1,)), ((), ())), preferred_element_type=F32)


def kernel(
    spaces,
    shots,
    steps,
    residual_hbm,
    codes,
    filter_hbm,
    offsets,
    z_high_hbm,
    z_low_hbm,
    across_hbm,
    rim_high_hbm,
    rim_low_hbm,
    now_hbm,
    previous_hbm,
    velocity_hbm,
    forward_hbm,
    gradient,
    last_hbm,
    residual,
    time_filter,
    z_high,
    z_low,
    across,
    rim_high,
    rim_low,
    q,
    high,
    low,
    speed,
    forward,
    image,
    source,
    gathered,
    halo_out,
    halo_in,
    stack_out,
    stack_in,
    local_sem,
    gather_send,
    gather_recv,
    halo_send,
    halo_recv,
    stack_send,
    stack_recv,
):
    cells = q.shape[1]
    chunks = cells // ROWS
    depth = q.shape[2]
    band = gradient.shape[0]
    lead = cells // CX // 4
    shot = lax.axis_index("shot")
    me = lax.axis_index("space")

    pairs = (
        (now_hbm, q.at[0]),
        (residual_hbm, residual),
        (filter_hbm, time_filter),
        (z_high_hbm, z_high),
        (z_low_hbm, z_low),
        (across_hbm, across),
        (rim_high_hbm, rim_high),
        (rim_low_hbm, rim_low),
        (previous_hbm, q.at[1]),
        (velocity_hbm, speed),
        (forward_hbm, forward),
    )
    loads = [
        pltpu.make_async_copy(there, here, local_sem.at[i]) for i, (there, here) in enumerate(pairs)
    ]
    for load in loads:
        load.start()

    barrier = pltpu.get_barrier_semaphore()
    for d in range(1, spaces):
        pl.semaphore_signal(
            barrier, inc=1, device_id=(shot, lax.rem(me + d, spaces)), device_id_type=MESH
        )
    for d in range(1, shots):
        pl.semaphore_signal(
            barrier, inc=1, device_id=(lax.rem(shot + d, shots), me), device_id_type=MESH
        )

    for slot in range(2):
        for piece in (high, low):
            piece[slot, 0:PAD, :] = jnp.zeros((PAD, depth), BF16)
            piece[slot, PAD + cells :, :] = jnp.zeros((PAD, depth), BF16)
    image[...] = jnp.zeros(image.shape, F32)

    has_left = me > 0
    has_right = me < spaces - 1

    @pl.when(jnp.logical_not(has_left))
    def _():
        halo_in[:, 0] = jnp.zeros((2,) + halo_in.shape[2:], F32)

    @pl.when(jnp.logical_not(has_right))
    def _():
        halo_in[:, 1] = jnp.zeros((2,) + halo_in.shape[2:], F32)

    pl.semaphore_wait(barrier, spaces - 1 + shots - 1)

    def gather_copy(d):
        return pltpu.make_async_remote_copy(
            src_ref=gathered.at[me],
            dst_ref=gathered.at[me],
            send_sem=gather_send.at[d - 1],
            recv_sem=gather_recv.at[d - 1],
            device_id=(shot, lax.rem(me + d, spaces)),
            device_id_type=MESH,
        )

    def gather_arrival(d):
        owner = lax.rem(me + spaces - d, spaces)
        return pltpu.make_async_remote_copy(
            src_ref=gathered.at[owner],
            dst_ref=gathered.at[owner],
            send_sem=gather_send.at[d - 1],
            recv_sem=gather_recv.at[d - 1],
            device_id=(shot, lax.rem(me + d, spaces)),
            device_id_type=MESH,
        )

    def halo_copy(slot, side, c):
        target = me - 1 if side == 0 else me + 1
        rows = pl.ds(c * EDGE, EDGE)
        return pltpu.make_async_remote_copy(
            src_ref=halo_out.at[slot, side, rows],
            dst_ref=halo_in.at[slot, 1 - side, rows],
            send_sem=halo_send.at[slot, side, c],
            recv_sem=halo_recv.at[slot, 1 - side, c],
            device_id=(shot, target),
            device_id_type=MESH,
        )

    def halo_arrival(slot, side, c):
        target = me - 1 if side == 0 else me + 1
        rows = pl.ds(c * EDGE, EDGE)
        return pltpu.make_async_remote_copy(
            src_ref=halo_out.at[slot, side, rows],
            dst_ref=halo_in.at[slot, side, rows],
            send_sem=halo_send.at[slot, side, c],
            recv_sem=halo_recv.at[slot, side, c],
            device_id=(shot, target),
            device_id_type=MESH,
        )

    first_half = lax.broadcasted_iota(jnp.int32, (8, depth), 0) < 4

    def publish_edges(slot, c, value):
        for pair in range(CHUNK_Y // 2):
            base = pair * 2 * CX
            low_a = value[base : base + 8]
            high_a = value[base + 8 : base + 16]
            low_b = value[base + 16 : base + 24]
            high_b = value[base + 24 : base + 32]
            at = pl.ds(c * EDGE + pair * 8, 8)
            halo_out[slot, 0, at, :] = jnp.where(first_half, low_a, pltpu.roll(low_b, 4, 0))
            halo_out[slot, 1, at, :] = jnp.where(first_half, pltpu.roll(high_a, 4, 0), high_b)

        @pl.when(has_left)
        def _():
            halo_copy(slot, 0, c).start()

        @pl.when(has_right)
        def _():
            halo_copy(slot, 1, c).start()

    def wait_edges_sent(slot, c):
        @pl.when(has_left)
        def _():
            halo_copy(slot, 0, c).wait_send()

        @pl.when(has_right)
        def _():
            halo_copy(slot, 1, c).wait_send()

    def publish_pieces(slot, c, value):
        value_high, value_low = split(value)
        high[slot, pl.ds(PAD + c * ROWS, ROWS), :] = value_high
        low[slot, pl.ds(PAD + c * ROWS, ROWS), :] = value_low

    loads[0].wait()
    for c in range(chunks):
        publish_edges(0, c, q[0, pl.ds(c * ROWS, ROWS), :])
    loads[1].wait()
    loads[2].wait()
    gathered[me, 0:8, :] = jnp.zeros((8, gathered.shape[2]), F32)
    gathered[me, 0:steps, :] = dot_nt(time_filter[...], residual[...])
    gathered[me, 6:7, :] = codes[...]
    for d in range(1, spaces):
        gather_copy(d).start()
    for c in range(chunks):
        publish_pieces(0, c, q[0, pl.ds(c * ROWS, ROWS), :])

    for d in range(1, spaces):
        gather_arrival(d).wait_recv()
    first_cell = (me * cells).astype(F32)

    def add_block(j, totals):
        block = gathered[j]
        block_high = block.astype(BF16).astype(F32)
        stacked = jnp.concatenate(
            [block_high, block - block_high, jnp.zeros((112, block.shape[1]), F32)], axis=0
        ).astype(BF16)
        wanted = block[6:7, :] - first_cell
        for c in range(chunks):
            cell = (lax.broadcasted_iota(jnp.int32, (ROWS, block.shape[1]), 0) + c * ROWS).astype(F32)
            hot = jnp.where(wanted == cell, 1.0, 0.0).astype(BF16)
            source[pl.ds(c * ROWS, ROWS), :] += dot_nt(hot, stacked)
        return totals

    source[...] = jnp.zeros(source.shape, F32)
    lax.fori_loop(0, spaces, add_block, 0)
    source[...] = source[...] + pltpu.roll(source[...], 120, 1)

    for load in loads[3:]:
        load.wait()

    first_lane = lax.broadcasted_iota(jnp.int32, (ROWS, 128), 1) == 0

    def step(k, carry):
        slot = lax.rem(k, 2)
        other = 1 - slot
        for c in range(chunks):
            rows = pl.ds(c * ROWS, ROWS)
            mid_high = high[slot, pl.ds(PAD + c * ROWS, ROWS), :]
            mid_low = low[slot, pl.ds(PAD + c * ROWS, ROWS), :]
            spread = dot(mid_high, z_high[...]) + dot(mid_high, z_low[...])
            spread = spread + dot(mid_low, z_high[...])
            parts = []
            for sub in range(2):
                window = pl.ds((2 * c + sub) * 128, 256)
                both = dot(across[...], high[slot, window, :])
                parts.append(both[:128] + both[128:] + dot(across[0:128], low[slot, window, :]))
            spread = spread + jnp.concatenate(parts, axis=0)

            @pl.when(has_left)
            def _():
                halo_arrival(slot, 0, c).wait_recv()

            @pl.when(has_right)
            def _():
                halo_arrival(slot, 1, c).wait_recv()

            at = pl.ds(c * EDGE, EDGE)
            rim = jnp.concatenate([halo_in[slot, 0, at, :], halo_in[slot, 1, at, :]], axis=0)
            rim_h, rim_l = split(rim)
            spread = spread + dot(rim_high[...], jnp.concatenate([rim_h, rim_l], axis=0))
            spread = spread + dot(rim_low[...], rim_h)

            value = 2.0 * q[slot, rows, :] - q[other, rows, :] + speed[rows, :] * spread
            added = source[rows, :]
            first = value[:, :128] + jnp.where(first_lane, added, 0.0)
            source[rows, :] = pltpu.roll(added, 127, 1)
            value = jnp.concatenate([first, value[:, 128:]], axis=1)
            q[other, rows, :] = value

            @pl.when(k < steps - 1)
            def _():
                @pl.when(k >= 1)
                def _():
                    wait_edges_sent(other, c)

                publish_edges(other, c, value)
                publish_pieces(other, c, value)

            inside = pl.ds(lead + c * CHUNK_Y, CHUNK_Y)
            product = forward[k, rows, :].astype(F32) * value
            image[inside] += product.reshape(CHUNK_Y, CX, depth)
        return carry

    lax.fori_loop(0, steps, step, 0)
    result = pltpu.make_async_copy(q.at[steps % 2], last_hbm, local_sem.at[0])
    result.start()

    moved = offsets[0]
    band_y = band // CX

    def shift_into(place, owner):
        for y in range(band_y):
            place[pl.ds(y * CX, CX), :] = image[owner * band_y + y - moved + lead]

    copies = []
    for d in range(1, shots):
        target = lax.rem(shot + d, shots)
        shift_into(stack_out.at[d - 1], target)
        copy = pltpu.make_async_remote_copy(
            src_ref=stack_out.at[d - 1],
            dst_ref=stack_in.at[d - 1],
            send_sem=stack_send.at[d - 1],
            recv_sem=stack_recv.at[d - 1],
            device_id=(target, me),
            device_id_type=MESH,
        )
        copy.start()
        copies.append(copy)
    shift_into(gradient, shot)
    for d in range(1, spaces):
        gather_copy(d).wait_send()
    for slot in range(2):
        for c in range(chunks):
            wait_edges_sent(slot, c)
    for d, copy in enumerate(copies):
        copy.wait_recv()
        gradient[...] += stack_in[d]
    for copy in copies:
        copy.wait_send()
    result.wait()


def local(
    spaces,
    shots,
    residual,
    record_tile,
    record_cell,
    time_filter,
    offsets,
    velocity,
    adjoint_prev,
    adjoint_now,
    forward_accel,
):
    _, ny, cx, depth = velocity.shape
    steps = forward_accel.shape[1]
    cells = ny * cx
    records = residual.shape[1]
    grid_y = ny + ny // 4
    band = grid_y // shots * cx
    chunks = cells // ROWS
    codes = (record_tile[0, :, 0] * cells + record_cell[0]).astype(F32)[None]
    constants = [jnp.asarray(matrix) for matrix in matrices(depth)]
    vmem = pl.BlockSpec(memory_space=pltpu.VMEM)
    there = pl.BlockSpec(memory_space=pltpu.HBM)
    gradient, last = pl.pallas_call(
        functools.partial(kernel, spaces, shots, steps),
        out_shape=(
            jax.ShapeDtypeStruct((band, depth), F32),
            jax.ShapeDtypeStruct((cells, depth), F32),
        ),
        in_specs=[there, vmem, there, pl.BlockSpec(memory_space=pltpu.SMEM)] + [there] * 9,
        out_specs=(vmem, pl.BlockSpec(memory_space=pl.ANY)),
        scratch_shapes=[
            pltpu.VMEM((records, residual.shape[2]), BF16),
            pltpu.VMEM(time_filter.shape, BF16),
            *[pltpu.VMEM(matrix.shape, BF16) for matrix in constants],
            pltpu.VMEM((2, cells, depth), F32),
            pltpu.VMEM((2, cells + 2 * PAD, depth), BF16),
            pltpu.VMEM((2, cells + 2 * PAD, depth), BF16),
            pltpu.VMEM((cells, depth), F32),
            pltpu.VMEM((steps, cells, depth), BF16),
            pltpu.VMEM((ny + 2 * (ny // 4), cx, depth), F32),
            pltpu.VMEM((cells, 128), F32),
            pltpu.VMEM((spaces, 8, records), F32),
            pltpu.VMEM((2, 2, chunks * EDGE, depth), F32),
            pltpu.VMEM((2, 2, chunks * EDGE, depth), F32),
            pltpu.VMEM((shots - 1, band, depth), F32),
            pltpu.VMEM((shots - 1, band, depth), F32),
            pltpu.SemaphoreType.DMA((11,)),
            pltpu.SemaphoreType.DMA((spaces - 1,)),
            pltpu.SemaphoreType.DMA((spaces - 1,)),
            pltpu.SemaphoreType.DMA((2, 2, chunks)),
            pltpu.SemaphoreType.DMA((2, 2, chunks)),
            pltpu.SemaphoreType.DMA((shots - 1,)),
            pltpu.SemaphoreType.DMA((shots - 1,)),
        ],
        compiler_params=pltpu.CompilerParams(
            collective_id=0, has_side_effects=True, vmem_limit_bytes=60 * 1024 * 1024
        ),
        cost_estimate=pl.CostEstimate(flops=6 * 10**9, bytes_accessed=8 * 10**6, transcendentals=0),
    )(
        residual[0],
        codes,
        time_filter,
        offsets,
        *constants,
        adjoint_now.reshape(cells, depth),
        adjoint_prev.reshape(cells, depth),
        velocity.reshape(cells, depth),
        forward_accel.reshape(steps, cells, depth),
    )
    return gradient.reshape(grid_y // shots, cx, depth), last.reshape(1, ny, cx, depth)


def solution(mesh):
    in_specs = (
        P("shot", "space", None),
        P("shot", "space", None),
        P("shot", "space"),
        P(),
        P("shot"),
        P("shot", None, "space", None),
        P("shot", None, "space", None),
        P("shot", None, "space", None),
        P("shot", None, None, "space", None),
    )
    out_specs = (P("shot", "space", None), P("shot", None, "space", None))
    body = functools.partial(local, mesh.shape["space"], mesh.shape["shot"])
    return jax.shard_map(body, mesh=mesh, in_specs=in_specs, out_specs=out_specs, check_vma=False)
```

```python
import functools

import jax
import jax.numpy as jnp
import numpy as np
from jax import lax
from jax.experimental import pallas as pl
from jax.experimental.pallas import tpu as pltpu
from jax.sharding import PartitionSpec as P

STENCIL = (-205.0 / 72.0, 8.0 / 5.0, -1.0 / 5.0, 8.0 / 315.0, -1.0 / 560.0)
MESH = pl.DeviceIdType.MESH
F32 = jnp.float32
BF16 = jnp.bfloat16
CX = 16
CHUNK_Y = 16
ROWS = CHUNK_Y * CX
EDGE = CHUNK_Y * 4
PAD = 64


def pieces(matrix):
    high = np.asarray(matrix, np.float32).astype(jnp.bfloat16)
    low = (matrix - high.astype(np.float64)).astype(np.float32).astype(jnp.bfloat16)
    return high, low


def coefficient(distance):
    distance = abs(distance)
    return STENCIL[distance] if 1 <= distance <= 4 else 0.0


def matrices(depth):
    along_z = np.zeros((depth, depth))
    for i in range(depth):
        along_z[i, i] = 3.0 * STENCIL[0]
        for j in range(max(0, i - 4), min(depth, i + 5)):
            if i != j:
                along_z[j, i] = coefficient(i - j)
    across = np.zeros((8 * CX, 16 * CX))
    for y in range(8):
        for x in range(CX):
            for other in range(16):
                across[y * CX + x, other * CX + x] += coefficient(other - 4 - y)
            for other in range(CX):
                across[y * CX + x, (y + 4) * CX + other] += coefficient(other - x)
    rim = np.zeros((ROWS, 2 * EDGE))
    for y in range(CHUNK_Y):
        for x in range(CX):
            for j in range(4):
                rim[y * CX + x, y * 4 + j] = coefficient(x + 4 - j)
                rim[y * CX + x, EDGE + y * 4 + j] = coefficient(16 + j - x)
    z_high, z_low = pieces(along_z)
    a_high, a_low = pieces(across)
    r_high, r_low = pieces(rim)
    return (
        np.concatenate([z_high, z_high, z_low], axis=0),
        np.concatenate([a_high, a_high, a_low], axis=1),
        np.concatenate([r_high, r_high, r_low], axis=1),
    )


def split(value):
    high = value.astype(BF16)
    low = (value - high.astype(F32)).astype(BF16)
    return high, low


def dot(a, b):
    return jnp.dot(a, b, preferred_element_type=F32)


def dot_nt(a, b):
    return lax.dot_general(a, b, (((1,), (1,)), ((), ())), preferred_element_type=F32)


def kernel(
    spaces,
    shots,
    steps,
    residual_hbm,
    codes,
    filter_hbm,
    offsets,
    along_z_hbm,
    across_hbm,
    rim_hbm,
    now_hbm,
    previous_hbm,
    velocity_hbm,
    forward_hbm,
    gradient,
    last_hbm,
    residual,
    time_filter,
    along_z,
    across,
    rim_matrix,
    q,
    high,
    low,
    speed,
    forward,
    image,
    source,
    gathered,
    halo_out,
    halo_in,
    stack_out,
    stack_in,
    local_sem,
    gather_send,
    gather_recv,
    halo_send,
    halo_recv,
    stack_send,
    stack_recv,
):
    cells = q.shape[1]
    chunks = cells // ROWS
    depth = q.shape[2]
    band = gradient.shape[0]
    lead = cells // CX // 4
    shot = lax.axis_index("shot")
    me = lax.axis_index("space")

    pairs = (
        (now_hbm, q.at[0]),
        (residual_hbm, residual),
        (filter_hbm, time_filter),
        (along_z_hbm, along_z),
        (across_hbm, across),
        (rim_hbm, rim_matrix),
        (previous_hbm, q.at[1]),
        (velocity_hbm, speed),
        (forward_hbm, forward),
    )
    loads = [
        pltpu.make_async_copy(there, here, local_sem.at[i]) for i, (there, here) in enumerate(pairs)
    ]
    for load in loads[:3]:
        load.start()

    barrier = pltpu.get_barrier_semaphore()
    for d in range(1, spaces):
        pl.semaphore_signal(
            barrier, inc=1, device_id=(shot, lax.rem(me + d, spaces)), device_id_type=MESH
        )
    for d in range(1, shots):
        pl.semaphore_signal(
            barrier, inc=1, device_id=(lax.rem(shot + d, shots), me), device_id_type=MESH
        )

    for slot in range(2):
        for piece in (high, low):
            piece[slot, 0:PAD, :] = jnp.zeros((PAD, depth), BF16)
            piece[slot, PAD + cells :, :] = jnp.zeros((PAD, depth), BF16)
    image[...] = jnp.zeros(image.shape, F32)

    has_left = me > 0
    has_right = me < spaces - 1

    @pl.when(jnp.logical_not(has_left))
    def _():
        halo_in[:, 0] = jnp.zeros((2,) + halo_in.shape[2:], F32)

    @pl.when(jnp.logical_not(has_right))
    def _():
        halo_in[:, 1] = jnp.zeros((2,) + halo_in.shape[2:], F32)

    pl.semaphore_wait(barrier, spaces - 1 + shots - 1)

    def gather_copy(d):
        return pltpu.make_async_remote_copy(
            src_ref=gathered.at[me],
            dst_ref=gathered.at[me],
            send_sem=gather_send.at[d - 1],
            recv_sem=gather_recv.at[d - 1],
            device_id=(shot, lax.rem(me + d, spaces)),
            device_id_type=MESH,
        )

    def gather_arrival(d):
        owner = lax.rem(me + spaces - d, spaces)
        return pltpu.make_async_remote_copy(
            src_ref=gathered.at[owner],
            dst_ref=gathered.at[owner],
            send_sem=gather_send.at[d - 1],
            recv_sem=gather_recv.at[d - 1],
            device_id=(shot, lax.rem(me + d, spaces)),
            device_id_type=MESH,
        )

    def halo_copy(slot, side, c):
        target = me - 1 if side == 0 else me + 1
        rows = pl.ds(c * EDGE, EDGE)
        return pltpu.make_async_remote_copy(
            src_ref=halo_out.at[slot, side, rows],
            dst_ref=halo_in.at[slot, 1 - side, rows],
            send_sem=halo_send.at[slot, side, c],
            recv_sem=halo_recv.at[slot, 1 - side, c],
            device_id=(shot, target),
            device_id_type=MESH,
        )

    def halo_arrival(slot, side, c):
        target = me - 1 if side == 0 else me + 1
        rows = pl.ds(c * EDGE, EDGE)
        return pltpu.make_async_remote_copy(
            src_ref=halo_out.at[slot, side, rows],
            dst_ref=halo_in.at[slot, side, rows],
            send_sem=halo_send.at[slot, side, c],
            recv_sem=halo_recv.at[slot, side, c],
            device_id=(shot, target),
            device_id_type=MESH,
        )

    first_half = lax.broadcasted_iota(jnp.int32, (8, depth), 0) < 4

    def publish_edges(slot, c, value):
        for pair in range(CHUNK_Y // 2):
            base = pair * 2 * CX
            low_a = value[base : base + 8]
            high_a = value[base + 8 : base + 16]
            low_b = value[base + 16 : base + 24]
            high_b = value[base + 24 : base + 32]
            at = pl.ds(c * EDGE + pair * 8, 8)
            halo_out[slot, 0, at, :] = jnp.where(first_half, low_a, pltpu.roll(low_b, 4, 0))
            halo_out[slot, 1, at, :] = jnp.where(first_half, pltpu.roll(high_a, 4, 0), high_b)

        @pl.when(has_left)
        def _():
            halo_copy(slot, 0, c).start()

        @pl.when(has_right)
        def _():
            halo_copy(slot, 1, c).start()

    def wait_edges_sent(slot, c):
        @pl.when(has_left)
        def _():
            halo_copy(slot, 0, c).wait_send()

        @pl.when(has_right)
        def _():
            halo_copy(slot, 1, c).wait_send()

    def publish_pieces(slot, c, value):
        value_high, value_low = split(value)
        high[slot, pl.ds(PAD + c * ROWS, ROWS), :] = value_high
        low[slot, pl.ds(PAD + c * ROWS, ROWS), :] = value_low

    loads[0].wait()
    for load in loads[3:]:
        load.start()
    for c in range(chunks):
        publish_edges(0, c, q[0, pl.ds(c * ROWS, ROWS), :])
    loads[1].wait()
    loads[2].wait()
    gathered[me, 0:8, :] = jnp.zeros((8, gathered.shape[2]), F32)
    gathered[me, 0:steps, :] = dot_nt(time_filter[...], residual[...])
    gathered[me, 6:7, :] = codes[...]
    for d in range(1, spaces):
        gather_copy(d).start()
    for c in range(chunks):
        publish_pieces(0, c, q[0, pl.ds(c * ROWS, ROWS), :])

    first_cell = (me * cells).astype(F32)

    def add_block(d, totals):
        @pl.when(d > 0)
        def _():
            gather_arrival(d).wait_recv()

        block = gathered[lax.rem(me + spaces - d, spaces)]
        block_high = block.astype(BF16).astype(F32)
        stacked = jnp.concatenate(
            [block_high, block - block_high, jnp.zeros((112, block.shape[1]), F32)], axis=0
        ).astype(BF16)
        wanted = block[6:7, :] - first_cell
        for c in range(chunks):
            cell = (lax.broadcasted_iota(jnp.int32, (ROWS, block.shape[1]), 0) + c * ROWS).astype(F32)
            hot = jnp.where(wanted == cell, 1.0, 0.0).astype(BF16)
            source[pl.ds(c * ROWS, ROWS), :] += dot_nt(hot, stacked)
        return totals

    source[...] = jnp.zeros(source.shape, F32)
    lax.fori_loop(0, spaces, add_block, 0)
    source[...] = source[...] + pltpu.roll(source[...], 120, 1)

    for load in loads[3:-1]:
        load.wait()

    first_lane = lax.broadcasted_iota(jnp.int32, (ROWS, 128), 1) == 0

    def step(k, carry):
        slot = lax.rem(k, 2)
        other = 1 - slot
        for c in range(chunks):
            rows = pl.ds(c * ROWS, ROWS)
            mid_high = high[slot, pl.ds(PAD + c * ROWS, ROWS), :]
            mid_low = low[slot, pl.ds(PAD + c * ROWS, ROWS), :]
            spread = dot(jnp.concatenate([mid_high, mid_low, mid_high], axis=1), along_z[...])
            parts = []
            for sub in range(2):
                window = pl.ds((2 * c + sub) * 128, 256)
                near = high[slot, window, :]
                stacked = jnp.concatenate([near, low[slot, window, :], near], axis=0)
                parts.append(dot(across[...], stacked))
            spread = spread + jnp.concatenate(parts, axis=0)

            @pl.when(has_left)
            def _():
                halo_arrival(slot, 0, c).wait_recv()

            @pl.when(has_right)
            def _():
                halo_arrival(slot, 1, c).wait_recv()

            at = pl.ds(c * EDGE, EDGE)
            rim = jnp.concatenate([halo_in[slot, 0, at, :], halo_in[slot, 1, at, :]], axis=0)
            rim_h, rim_l = split(rim)
            spread = spread + dot(rim_matrix[...], jnp.concatenate([rim_h, rim_l, rim_h], axis=0))

            value = 2.0 * q[slot, rows, :] - q[other, rows, :] + speed[rows, :] * spread
            added = source[rows, :]
            first = value[:, :128] + jnp.where(first_lane, added, 0.0)
            source[rows, :] = pltpu.roll(added, 127, 1)
            value = jnp.concatenate([first, value[:, 128:]], axis=1)
            q[other, rows, :] = value

            @pl.when(k < steps - 1)
            def _():
                @pl.when(k >= 1)
                def _():
                    wait_edges_sent(other, c)

                publish_edges(other, c, value)
                publish_pieces(other, c, value)

            if c == 0:

                @pl.when(k == 0)
                def _():
                    loads[-1].wait()

            inside = pl.ds(lead + c * CHUNK_Y, CHUNK_Y)
            product = forward[k, rows, :].astype(F32) * value
            image[inside] += product.reshape(CHUNK_Y, CX, depth)
        return carry

    lax.fori_loop(0, steps, step, 0)
    result = pltpu.make_async_copy(q.at[steps % 2], last_hbm, local_sem.at[0])
    result.start()

    moved = offsets[0]
    band_y = band // CX

    def shift_into(place, owner):
        for y in range(band_y):
            place[pl.ds(y * CX, CX), :] = image[owner * band_y + y - moved + lead]

    copies = []
    for d in range(1, shots):
        target = lax.rem(shot + d, shots)
        shift_into(stack_out.at[d - 1], target)
        copy = pltpu.make_async_remote_copy(
            src_ref=stack_out.at[d - 1],
            dst_ref=stack_in.at[d - 1],
            send_sem=stack_send.at[d - 1],
            recv_sem=stack_recv.at[d - 1],
            device_id=(target, me),
            device_id_type=MESH,
        )
        copy.start()
        copies.append(copy)
    shift_into(gradient, shot)
    for d in range(1, spaces):
        gather_copy(d).wait_send()
    for slot in range(2):
        for c in range(chunks):
            wait_edges_sent(slot, c)
    for d, copy in enumerate(copies):
        copy.wait_recv()
        gradient[...] += stack_in[d]
    for copy in copies:
        copy.wait_send()
    result.wait()


def local(
    spaces,
    shots,
    residual,
    record_tile,
    record_cell,
    time_filter,
    offsets,
    velocity,
    adjoint_prev,
    adjoint_now,
    forward_accel,
):
    _, ny, cx, depth = velocity.shape
    steps = forward_accel.shape[1]
    cells = ny * cx
    records = residual.shape[1]
    grid_y = ny + ny // 4
    band = grid_y // shots * cx
    chunks = cells // ROWS
    codes = (record_tile[0, :, 0] * cells + record_cell[0]).astype(F32)[None]
    constants = [jnp.asarray(matrix) for matrix in matrices(depth)]
    vmem = pl.BlockSpec(memory_space=pltpu.VMEM)
    there = pl.BlockSpec(memory_space=pltpu.HBM)
    gradient, last = pl.pallas_call(
        functools.partial(kernel, spaces, shots, steps),
        out_shape=(
            jax.ShapeDtypeStruct((band, depth), F32),
            jax.ShapeDtypeStruct((cells, depth), F32),
        ),
        in_specs=[there, vmem, there, pl.BlockSpec(memory_space=pltpu.SMEM)] + [there] * 7,
        out_specs=(vmem, pl.BlockSpec(memory_space=pl.ANY)),
        scratch_shapes=[
            pltpu.VMEM((records, residual.shape[2]), BF16),
            pltpu.VMEM(time_filter.shape, BF16),
            *[pltpu.VMEM(matrix.shape, BF16) for matrix in constants],
            pltpu.VMEM((2, cells, depth), F32),
            pltpu.VMEM((2, cells + 2 * PAD, depth), BF16),
            pltpu.VMEM((2, cells + 2 * PAD, depth), BF16),
            pltpu.VMEM((cells, depth), F32),
            pltpu.VMEM((steps, cells, depth), BF16),
            pltpu.VMEM((ny + 2 * (ny // 4), cx, depth), F32),
            pltpu.VMEM((cells, 128), F32),
            pltpu.VMEM((spaces, 8, records), F32),
            pltpu.VMEM((2, 2, chunks * EDGE, depth), F32),
            pltpu.VMEM((2, 2, chunks * EDGE, depth), F32),
            pltpu.VMEM((shots - 1, band, depth), F32),
            pltpu.VMEM((shots - 1, band, depth), F32),
            pltpu.SemaphoreType.DMA((9,)),
            pltpu.SemaphoreType.DMA((spaces - 1,)),
            pltpu.SemaphoreType.DMA((spaces - 1,)),
            pltpu.SemaphoreType.DMA((2, 2, chunks)),
            pltpu.SemaphoreType.DMA((2, 2, chunks)),
            pltpu.SemaphoreType.DMA((shots - 1,)),
            pltpu.SemaphoreType.DMA((shots - 1,)),
        ],
        compiler_params=pltpu.CompilerParams(
            collective_id=0, has_side_effects=True, vmem_limit_bytes=60 * 1024 * 1024
        ),
        cost_estimate=pl.CostEstimate(flops=6 * 10**9, bytes_accessed=8 * 10**6, transcendentals=0),
    )(
        residual[0],
        codes,
        time_filter,
        offsets,
        *constants,
        adjoint_now.reshape(cells, depth),
        adjoint_prev.reshape(cells, depth),
        velocity.reshape(cells, depth),
        forward_accel.reshape(steps, cells, depth),
    )
    return gradient.reshape(grid_y // shots, cx, depth), last.reshape(1, ny, cx, depth)


def solution(mesh):
    in_specs = (
        P("shot", "space", None),
        P("shot", "space", None),
        P("shot", "space"),
        P(),
        P("shot"),
        P("shot", None, "space", None),
        P("shot", None, "space", None),
        P("shot", None, "space", None),
        P("shot", None, None, "space", None),
    )
    out_specs = (P("shot", "space", None), P("shot", None, "space", None))
    body = functools.partial(local, mesh.shape["space"], mesh.shape["shot"])
    return jax.shard_map(body, mesh=mesh, in_specs=in_specs, out_specs=out_specs, check_vma=False)
```
